256 devices in a mesh: rep: 16 (over z_lo, y, core), fsdp: 16 (over x, z_hi).
Axes of the slice: x: 4, y: 4, z: 8 (z_hi: 4, z_lo: 2; z = z_hi * 2 + z_lo), core: 2. Of those that a mesh axis runs over, the one named last changes fastest.
Arguments:
- activations: bfloat16 [131072, 5120], P(('rep', 'fsdp')), may hold values from -6 to 6
- cotangent: bfloat16 [131072, 512], P(('rep', 'fsdp')), may hold values from -6 to 6
- inner_weights: float32 [16, 5120, 512], P('rep', 'fsdp'), may hold values from -10 to 10
- adam_m: float32 [16, 5120, 512], P('rep', 'fsdp'), may hold values from -6 to 6
- adam_v: float32 [16, 5120, 512], P('rep', 'fsdp'), may hold values from 0.05 to 2
- anchor: float32 [5120, 512], P('fsdp'), may hold values from -6 to 6
- momentum: float32 [5120, 512], P('fsdp'), may hold values from -2 to 2
- fragment: int32 [4], replicated, may hold values from 0 to 3, each once
Outputs:
- new_weights: float32 [16, 5120, 512], P('rep', 'fsdp')
- new_momentum: float32 [5120, 512], P('fsdp')
The draws below stay inside these ranges and needn't reach their ends.
All inputs are finite; a program needn't handle non-finite values.
Results may differ from the reference program's by a relative error of at most 0.00075.
Values may be sent and summed in bfloat16 or wider, within the bound.
No kernel may reach another device: no remote copies, remote signals or barrier semaphores. Data moves between devices by JAX's collectives and lax.ppermute only.
A program may use at most 128 MiB of HBM per device.

```python
import math
import jax
import jax.numpy as jnp
from jax import lax

D = 5120
HEAD_DIM = 128
KV_HEADS = 4
KV = 512
TOK_DEV = 512
REPS = 16
TOKENS = 131072
N_REP = 16
N_FSDP = 16


def anchor_field(key):
    field = jnp.clip(jax.random.normal(jax.random.fold_in(key, 7), (D, KV_HEADS * HEAD_DIM), jnp.float32), -6.0, 6.0)
    return field


def draw_anchor(key, part):
    field = anchor_field(key)
    return field


def draw_inner_weights(key, part):
    field = anchor_field(key)
    key = jax.random.fold_in(key, 5)
    ranks = jnp.arange(REPS, dtype=jnp.float32) / (REPS - 1)
    spread = 0.3 * (1.0 + 2.0 * ranks)
    noise = jax.random.normal(jax.random.fold_in(key, 1), (REPS, D, KV_HEADS * HEAD_DIM), jnp.float32)
    return jnp.clip(field[None] + spread[:, None, None] * noise, -10.0, 10.0)


def level_of(key, dims, cuts, low, high):
    def one(axis_at, blocks):
        steps = jax.random.uniform(jax.random.fold_in(jax.random.fold_in(key, 6), axis_at), (blocks,), jnp.float32, low / len(cuts), high / len(cuts))
        return jnp.repeat(jnp.exp(steps), dims[axis_at] // blocks).reshape((-1,) + (1,) * (len(dims) - axis_at - 1))

    factor_of = one(*cuts[0])
    for cut in cuts[1:]:
        factor_of = factor_of * one(*cut)
    return factor_of


def normal_values(own_key, shape, width, bound, shards=(), kind=jnp.bfloat16):
    drawn = jax.random.normal(own_key, shape, jnp.float32) * width
    if len(shards) > 0:
        drawn = level_of(own_key, shape, shards, -0.22, 0.18) * drawn
    return jnp.clip(drawn, min=-bound, max=bound).astype(kind)


def setup_inputs(seed: int = 0) -> dict:
    splits = jax.random.split(jax.random.key(seed), 9)
    activations = normal_values(splits[0], (TOKENS, D), 1.0, 6.0, ((0, 256),))
    cotangent = normal_values(splits[1], (TOKENS, KV), 1.0, 6.0, ((0, 256),))
    inner_weights = draw_inner_weights(jax.random.fold_in(splits[8], 71), 0)
    adam_m = normal_values(splits[3], (REPS, D, KV), 1.0, 6.0, ((0, 16), (1, 16)), jnp.float32)
    adam_v = jnp.clip(jnp.exp(math.log(2.0) - 3.6888794 * jax.random.uniform(splits[4], (REPS, D, KV), jnp.float32) ** level_of(splits[4], (REPS, D, KV), ((0, 16), (1, 16)), -0.2, 0.2)), 0.05, 2.0)
    anchor = draw_anchor(jax.random.fold_in(splits[8], 71), 0)
    momentum = normal_values(splits[6], (D, KV), 0.3, 2.0, ((0, 16),), jnp.float32)
    fragment = jax.random.permutation(splits[7], KV_HEADS).astype(jnp.int32)
    return {"activations": activations, "cotangent": cotangent, "inner_weights": inner_weights, "adam_m": adam_m, "adam_v": adam_v, "anchor": anchor, "momentum": momentum, "fragment": fragment}


beta_first = 0.9
beta_second = 0.95
inner_rate = 0.1
decay_rate = 0.1
adam_epsilon = 1e-08
norm_epsilon = 1e-06
outer_rate = 0.7
nesterov = 0.9
mixing = 0.5

def outer_update(held, carried, total, replicas):
    delta = held - total / replicas
    carried = nesterov * carried + delta
    return (held - outer_rate * (delta + nesterov * carried), carried)

def normalize_back(keys, cotangent):
    scale = jnp.sqrt(lax.optimization_barrier(jnp.mean(keys * keys, -1, keepdims=True)) + norm_epsilon)
    normed = keys / scale
    upstream = cotangent.astype(jnp.float32)
    inner = lax.optimization_barrier(jnp.mean(upstream * normed, -1, keepdims=True))
    return ((upstream - normed * inner) / scale).astype(jnp.bfloat16)

def adamw(weight, first, second, grad):
    first = beta_first * first + (1.0 - beta_first) * grad
    second = beta_second * second + (1.0 - beta_second) * grad * grad
    weight = weight - inner_rate * (first / (jnp.sqrt(second) + adam_epsilon) + decay_rate * weight)
    return (weight, first, second)

def inner_step(tokens, cotangent, weight, first, second):
    keys = jnp.dot(tokens, weight.astype(jnp.bfloat16), preferred_element_type=jnp.float32)
    key_grad = normalize_back(keys, cotangent)
    blocks = tokens.reshape(N_FSDP, TOK_DEV, D).astype(jnp.float32)
    grads = key_grad.reshape(N_FSDP, TOK_DEV, KV).astype(jnp.float32)
    parts = jnp.einsum('std,stk->sdk', blocks, grads)
    rounded = lax.optimization_barrier(parts.astype(jnp.bfloat16))
    grad = lax.optimization_barrier(jnp.sum(rounded.astype(jnp.float32), 0))
    return adamw(weight, first, second, grad)

def reference(activations, cotangent, inner_weights, adam_m, adam_v, anchor, momentum, fragment):
    start_first = fragment[0].astype(jnp.int32) * HEAD_DIM
    start_second = fragment[1].astype(jnp.int32) * HEAD_DIM
    own = jnp.concatenate([lax.dynamic_slice_in_dim(inner_weights, start_first, HEAD_DIM, 2), lax.dynamic_slice_in_dim(inner_weights, start_second, HEAD_DIM, 2)], 2)
    total = lax.optimization_barrier(jnp.sum(own, 0))
    held = jnp.concatenate([lax.dynamic_slice_in_dim(anchor, start_first, HEAD_DIM, 1), lax.dynamic_slice_in_dim(anchor, start_second, HEAD_DIM, 1)], 1)
    carried = jnp.concatenate([lax.dynamic_slice_in_dim(momentum, start_first, HEAD_DIM, 1), lax.dynamic_slice_in_dim(momentum, start_second, HEAD_DIM, 1)], 1)
    new_anchor, new_carried = outer_update(held, carried, total, N_REP)
    tokens = activations.reshape(N_REP, N_FSDP * TOK_DEV, D)
    upstream = cotangent.reshape(N_REP, N_FSDP * TOK_DEV, KV)

    def replica(items):
        tok, cot, weight, first, second = items
        weight, first, second = inner_step(tok, cot, weight, first, second)
        mixed = mixing * lax.dynamic_slice_in_dim(weight, start_first, HEAD_DIM, 1) + (1.0 - mixing) * new_anchor[:, :HEAD_DIM]
        weight = lax.dynamic_update_slice_in_dim(weight, mixed, start_first, 1)
        weight, first, second = inner_step(tok, cot, weight, first, second)
        mixed = mixing * lax.dynamic_slice_in_dim(weight, start_second, HEAD_DIM, 1) + (1.0 - mixing) * new_anchor[:, HEAD_DIM:]
        return lax.dynamic_update_slice_in_dim(weight, mixed, start_second, 1)
    new_weights = lax.map(replica, (tokens, upstream, inner_weights, adam_m, adam_v))
    new_momentum = lax.dynamic_update_slice_in_dim(momentum, new_carried[:, :HEAD_DIM], start_first, 1)
    new_momentum = lax.dynamic_update_slice_in_dim(new_momentum, new_carried[:, HEAD_DIM:], start_second, 1)
    return (new_weights, new_momentum)
```

```python
import jax
import jax.numpy as jnp
from jax import lax
from jax.sharding import PartitionSpec as P

HEAD_DIM = 128
SIDE = 4


beta_first = 0.9
beta_second = 0.95
inner_rate = 0.1
decay_rate = 0.1
adam_epsilon = 1e-08
norm_epsilon = 1e-06
outer_rate = 0.7
nesterov = 0.9
mixing = 0.5


def outer_update(held, carried, total, replicas):
    delta = held - total / replicas
    carried = nesterov * carried + delta
    return (held - outer_rate * (delta + nesterov * carried), carried)


def normalize_back(keys, cotangent):
    scale = jnp.sqrt(jnp.mean(keys * keys, -1, keepdims=True) + norm_epsilon)
    normed = keys / scale
    upstream = cotangent.astype(jnp.float32)
    inner = jnp.mean(upstream * normed, -1, keepdims=True)
    return ((upstream - normed * inner) / scale).astype(jnp.bfloat16)


def adamw(weight, first, second, grad):
    first = beta_first * first + (1.0 - beta_first) * grad
    second = beta_second * second + (1.0 - beta_second) * grad * grad
    weight = weight - inner_rate * (first / (jnp.sqrt(second) + adam_epsilon) + decay_rate * weight)
    return (weight, first, second)


def two_blocks(source, start_first, start_second):
    return jnp.concatenate(
        [
            lax.dynamic_slice_in_dim(source, start_first, HEAD_DIM, 1),
            lax.dynamic_slice_in_dim(source, start_second, HEAD_DIM, 1),
        ],
        1,
    )


def shift(value, along, step):
    pairs = []
    for index in range(SIDE * SIDE):
        x, z = divmod(index, SIDE)
        if along == "x":
            x = (x + step) % SIDE
        else:
            z = (z + step) % SIDE
        pairs.append((index, x * SIDE + z))
    return lax.ppermute(value, "fsdp", pairs)


def sum_replicas(value):
    for bit in (1, 2, 4, 8):
        value = value + lax.ppermute(value, "rep", [(i, i ^ bit) for i in range(16)])
    return value


def gather_line(block, along):
    half = block.shape[0] // 2
    before = shift(block, along, 1)
    after = shift(block, along, -1)
    far = jnp.concatenate(
        [shift(before[:half], along, 1), shift(after[half:], along, -1)], 0
    )
    return after, before, far


def wide(value):
    return value.astype(jnp.float32)


def scatter_line(own, after, before, far, along):
    half = own.shape[0] // 2
    kind = own.dtype
    from_before = shift(far[:half], along, 1)
    from_after = shift(far[half:], along, -1)
    after = jnp.concatenate(
        [(wide(after[:half]) + wide(from_before)).astype(kind), after[half:]], 0
    )
    before = jnp.concatenate(
        [before[:half], (wide(before[half:]) + wide(from_after)).astype(kind)], 0
    )
    return wide(own) + wide(shift(after, along, 1)) + wide(shift(before, along, -1))


def shards(activations, cotangent, inner_weights, adam_m, adam_v, anchor, momentum, fragment):
    weight = inner_weights[0]
    first = adam_m[0]
    second = adam_v[0]
    rows = weight.shape[0]
    start_first = fragment[0] * HEAD_DIM
    start_second = fragment[1] * HEAD_DIM
    replicas = lax.axis_size("rep")
    place = lax.axis_index("fsdp")
    at_x = place // SIDE
    at_z = place % SIDE
    order = (0, 1, -1, 2)

    def block_at(source, step_x, step_z):
        x = (at_x + step_x + SIDE) % SIDE
        z = (at_z + step_z + SIDE) % SIDE
        return lax.dynamic_slice_in_dim(source, (x * SIDE + z) * rows, rows, 0)

    turned = lax.optimization_barrier(activations.T)
    chunks = [
        jnp.concatenate([block_at(turned, step_x, step_z) for step_x in order], 0)
        for step_z in order
    ]
    chunks = lax.optimization_barrier(chunks)

    own = two_blocks(weight, start_first, start_second)
    held = two_blocks(anchor, start_first, start_second)
    carried = two_blocks(momentum, start_first, start_second)
    total = sum_replicas(own)
    new_anchor, new_carried = outer_update(held, carried, total, replicas)

    def inner_step(weight, first, second):
        working = weight.astype(jnp.bfloat16)
        blocks = (working,) + gather_line(working, "z")
        keys = 0.0
        for chunk, block in zip(chunks, blocks):
            whole = jnp.concatenate((block,) + gather_line(block, "x"), 0)
            keys = keys + lax.dot_general(
                chunk, whole, (((0,), (0,)), ((), ())), preferred_element_type=jnp.float32
            )
        key_grad = normalize_back(keys, cotangent)
        sums = []
        for chunk in (chunks[3], chunks[1], chunks[2], chunks[0]):
            part = jnp.dot(chunk, key_grad, preferred_element_type=jnp.float32)
            part = part.astype(jnp.bfloat16).reshape(SIDE, rows, -1)
            sums.append(scatter_line(part[0], part[1], part[2], part[3], "x"))
        far, after, before, own = [part.astype(jnp.bfloat16) for part in sums]
        grad = scatter_line(own, after, before, far, "z")
        return adamw(weight, first, second, grad)

    weight, first, second = inner_step(weight, first, second)
    mixed = (
        mixing * lax.dynamic_slice_in_dim(weight, start_first, HEAD_DIM, 1)
        + (1.0 - mixing) * new_anchor[:, :HEAD_DIM]
    )
    weight = lax.dynamic_update_slice_in_dim(weight, mixed, start_first, 1)
    weight, first, second = inner_step(weight, first, second)
    mixed = (
        mixing * lax.dynamic_slice_in_dim(weight, start_second, HEAD_DIM, 1)
        + (1.0 - mixing) * new_anchor[:, HEAD_DIM:]
    )
    weight = lax.dynamic_update_slice_in_dim(weight, mixed, start_second, 1)
    new_momentum = lax.dynamic_update_slice_in_dim(
        momentum, new_carried[:, :HEAD_DIM], start_first, 1
    )
    new_momentum = lax.dynamic_update_slice_in_dim(
        new_momentum, new_carried[:, HEAD_DIM:], start_second, 1
    )
    return (weight[None], new_momentum)


def solution(mesh):
    return jax.shard_map(
        shards,
        mesh=mesh,
        in_specs=(
            P(("rep", "fsdp"), None),
            P(("rep", "fsdp"), None),
            P("rep", "fsdp", None),
            P("rep", "fsdp", None),
            P("rep", "fsdp", None),
            P("fsdp", None),
            P("fsdp", None),
            P(),
        ),
        out_specs=(P("rep", "fsdp", None), P("fsdp", None)),
        check_vma=False,
    )
```

```python
import jax
import jax.numpy as jnp
from jax import lax
from jax.experimental import pallas as pl
from jax.experimental.pallas import tpu as pltpu
from jax.sharding import PartitionSpec as P

HEAD_DIM = 128
SIDE = 4


beta_first = 0.9
beta_second = 0.95
inner_rate = 0.1
decay_rate = 0.1
adam_epsilon = 1e-08
norm_epsilon = 1e-06
outer_rate = 0.7
nesterov = 0.9
mixing = 0.5


def outer_update(held, carried, total, replicas):
    delta = held - total / replicas
    carried = nesterov * carried + delta
    return (held - outer_rate * (delta + nesterov * carried), carried)


def normalize_back(keys, cotangent):
    scale = jnp.sqrt(jnp.mean(keys * keys, -1, keepdims=True) + norm_epsilon)
    normed = keys / scale
    upstream = cotangent.astype(jnp.float32)
    inner = jnp.mean(upstream * normed, -1, keepdims=True)
    return ((upstream - normed * inner) / scale).astype(jnp.bfloat16)


def adamw(weight, first, second, grad):
    first = beta_first * first + (1.0 - beta_first) * grad
    second = beta_second * second + (1.0 - beta_second) * grad * grad
    weight = weight - inner_rate * (first / (jnp.sqrt(second) + adam_epsilon) + decay_rate * weight)
    return (weight, first, second)


def two_blocks(source, start_first, start_second):
    return jnp.concatenate(
        [
            lax.dynamic_slice_in_dim(source, start_first, HEAD_DIM, 1),
            lax.dynamic_slice_in_dim(source, start_second, HEAD_DIM, 1),
        ],
        1,
    )


def swap(value, along, bits):
    step = bits * SIDE if along == "x" else bits
    return lax.ppermute(value, "fsdp", [(i, i ^ step) for i in range(SIDE * SIDE)])


def sum_replicas(value):
    for bit in (1, 2, 4, 8):
        value = value + lax.ppermute(value, "rep", [(i, i ^ bit) for i in range(16)])
    return value


def wide(value):
    return value.astype(jnp.float32)


def narrow(value):
    return value.astype(jnp.bfloat16)


def gather_line(block, along):
    half = block.shape[0] // 2
    one = swap(block, along, 1)
    three = swap(block, along, 3)
    two = jnp.concatenate([swap(three[:half], along, 1), swap(one[half:], along, 3)], 0)
    return one, three, two


def scatter_line(own, one, three, two, along):
    half = own.shape[0] // 2
    to_three = swap(two[:half], along, 1)
    to_one = swap(two[half:], along, 3)
    one = jnp.concatenate([one[:half], narrow(wide(one[half:]) + wide(to_one))], 0)
    three = jnp.concatenate([narrow(wide(three[:half]) + wide(to_three)), three[half:]], 0)
    return wide(own) + wide(swap(one, along, 1)) + wide(swap(three, along, 3))


def place_kernel(at_ref, source_ref, *chunk_refs):
    block = source_ref.shape[1] // (SIDE * SIDE)
    pair = 2 * block
    at_x = at_ref[0]
    at_z = at_ref[1]
    odd = at_z % 2
    for upper in range(2):
        for left, right in ((0, 1), (3, 2)):
            half = (at_z // 2) ^ upper
            spans = []
            for bits in (left, right):
                start = pl.multiple_of(((at_x ^ bits) * 2 + half) * pair, pair)
                spans.append(source_ref[:, pl.ds(start, pair)])
            evens = jnp.concatenate([span[:, :block] for span in spans], 1)
            odds = jnp.concatenate([span[:, block:] for span in spans], 1)
            to = pl.ds(0 if left == 0 else pair, pair)
            same, other = chunk_refs[2 * upper], chunk_refs[2 * upper + 1]

            @pl.when(odd == 0)
            def _():
                same[:, to] = evens
                other[:, to] = odds

            @pl.when(odd == 1)
            def _():
                same[:, to] = odds
                other[:, to] = evens


def place_chunks(at_x, at_z, source):
    tokens, width = source.shape
    whole = pl.BlockSpec(memory_space=pltpu.VMEM)
    return pl.pallas_call(
        place_kernel,
        out_shape=[jax.ShapeDtypeStruct((tokens, width // SIDE), source.dtype)] * SIDE,
        in_specs=[pl.BlockSpec(memory_space=pltpu.SMEM), whole],
        out_specs=[whole] * SIDE,
        compiler_params=pltpu.CompilerParams(vmem_limit_bytes=32 * 2**20),
        cost_estimate=pl.CostEstimate(
            flops=0, bytes_accessed=4 * tokens * width, transcendentals=0
        ),
    )(jnp.stack([at_x, at_z]).astype(jnp.int32), source)


def shards(activations, cotangent, inner_weights, adam_m, adam_v, anchor, momentum, fragment):
    weight = inner_weights[0]
    first = adam_m[0]
    second = adam_v[0]
    rows = weight.shape[0]
    start_first = fragment[0] * HEAD_DIM
    start_second = fragment[1] * HEAD_DIM
    replicas = lax.axis_size("rep")
    place = lax.axis_index("fsdp")
    at_x = place // SIDE
    at_z = place % SIDE
    working = weight.astype(jnp.bfloat16)
    working, activations, weight, anchor, momentum = lax.optimization_barrier(
        (working, activations, weight, anchor, momentum)
    )
    chunks = place_chunks(at_x, at_z, activations)

    own = two_blocks(weight, start_first, start_second)
    held = two_blocks(anchor, start_first, start_second)
    carried = two_blocks(momentum, start_first, start_second)
    total = sum_replicas(own)
    new_anchor, new_carried = outer_update(held, carried, total, replicas)

    def product(chunk, whole):
        return lax.dot_general(
            chunk, whole, (((1,), (0,)), ((), ())), preferred_element_type=jnp.float32
        )

    def part_of(chunk, key_grad):
        part = lax.dot_general(
            chunk, key_grad, (((0,), (0,)), ((), ())), preferred_element_type=jnp.float32
        )
        return narrow(part).reshape(SIDE, rows, -1)

    def inner_step(working, weight, first, second):
        near, wrap, far = gather_line(working, "z")
        keys = product(chunks[0], jnp.concatenate((working,) + gather_line(working, "x"), 0))
        both = jnp.concatenate([near, wrap], 0)
        one = swap(both, "x", 1)
        three = swap(both, "x", 3)
        two_near = swap(three[:rows], "x", 1)
        two_wrap = swap(one[rows:], "x", 3)
        keys = keys + product(
            chunks[1], jnp.concatenate([near, one[:rows], three[:rows], two_near], 0)
        )
        keys = keys + product(
            chunks[3], jnp.concatenate([wrap, one[rows:], three[rows:], two_wrap], 0)
        )
        keys = keys + product(chunks[2], jnp.concatenate((far,) + gather_line(far, "x"), 0))
        key_grad = normalize_back(keys, cotangent)
        part = part_of(chunks[2], key_grad)
        far = narrow(scatter_line(part[0], part[1], part[2], part[3], "x"))
        near = part_of(chunks[1], key_grad)
        wrap = part_of(chunks[3], key_grad)
        to_three = swap(near[3], "x", 1)
        to_one = swap(wrap[3], "x", 3)
        one = swap(
            jnp.concatenate([near[1], narrow(wide(wrap[1]) + wide(to_one))], 0), "x", 1
        )
        three = swap(
            jnp.concatenate([narrow(wide(near[2]) + wide(to_three)), wrap[2]], 0), "x", 3
        )
        near = narrow(wide(near[0]) + wide(one[:rows]) + wide(three[:rows]))
        wrap = narrow(wide(wrap[0]) + wide(one[rows:]) + wide(three[rows:]))
        part = part_of(chunks[0], key_grad)
        own = narrow(scatter_line(part[0], part[1], part[2], part[3], "x"))
        grad = scatter_line(own, near, wrap, far, "z")
        return adamw(weight, first, second, grad)

    weight, first, second = inner_step(working, weight, first, second)
    mixed = (
        mixing * lax.dynamic_slice_in_dim(weight, start_first, HEAD_DIM, 1)
        + (1.0 - mixing) * new_anchor[:, :HEAD_DIM]
    )
    weight = lax.dynamic_update_slice_in_dim(weight, mixed, start_first, 1)
    working = weight.astype(jnp.bfloat16)
    weight, first, second = inner_step(working, weight, first, second)
    mixed = (
        mixing * lax.dynamic_slice_in_dim(weight, start_second, HEAD_DIM, 1)
        + (1.0 - mixing) * new_anchor[:, HEAD_DIM:]
    )
    weight = lax.dynamic_update_slice_in_dim(weight, mixed, start_second, 1)
    new_momentum = lax.dynamic_update_slice_in_dim(
        momentum, new_carried[:, :HEAD_DIM], start_first, 1
    )
    new_momentum = lax.dynamic_update_slice_in_dim(
        new_momentum, new_carried[:, HEAD_DIM:], start_second, 1
    )
    return (weight[None], new_momentum)


def solution(mesh):
    return jax.shard_map(
        shards,
        mesh=mesh,
        in_specs=(
            P(("rep", "fsdp"), None),
            P(("rep", "fsdp"), None),
            P("rep", "fsdp", None),
            P("rep", "fsdp", None),
            P("rep", "fsdp", None),
            P("fsdp", None),
            P("fsdp", None),
            P(),
        ),
        out_specs=(P("rep", "fsdp", None), P("fsdp", None)),
        check_vma=False,
    )
```

```python
import jax
import jax.numpy as jnp
from jax import lax
from jax.experimental import pallas as pl
from jax.experimental.pallas import tpu as pltpu
from jax.sharding import PartitionSpec as P

HEAD_DIM = 128
SIDE = 4


beta_first = 0.9
beta_second = 0.95
inner_rate = 0.1
decay_rate = 0.1
adam_epsilon = 1e-08
norm_epsilon = 1e-06
outer_rate = 0.7
nesterov = 0.9
mixing = 0.5


def outer_update(held, carried, total, replicas):
    delta = held - total / replicas
    carried = nesterov * carried + delta
    return (held - outer_rate * (delta + nesterov * carried), carried)


def normalize_back(keys, cotangent):
    scale = jnp.sqrt(jnp.mean(keys * keys, -1, keepdims=True) + norm_epsilon)
    normed = keys / scale
    upstream = cotangent.astype(jnp.float32)
    inner = jnp.mean(upstream * normed, -1, keepdims=True)
    return ((upstream - normed * inner) / scale).astype(jnp.bfloat16)


def adamw(weight, first, second, grad):
    first = beta_first * first + (1.0 - beta_first) * grad
    second = beta_second * second + (1.0 - beta_second) * grad * grad
    weight = weight - inner_rate * (first / (jnp.sqrt(second) + adam_epsilon) + decay_rate * weight)
    return (weight, first, second)


def two_blocks(source, start_first, start_second):
    return jnp.concatenate(
        [
            lax.dynamic_slice_in_dim(source, start_first, HEAD_DIM, 1),
            lax.dynamic_slice_in_dim(source, start_second, HEAD_DIM, 1),
        ],
        1,
    )


def swap(value, along, bits):
    step = bits * SIDE if along == "x" else bits
    return lax.ppermute(value, "fsdp", [(i, i ^ step) for i in range(SIDE * SIDE)])


def shift(value, step):
    count = SIDE * SIDE
    return lax.ppermute(value, "fsdp", [(i, (i + step * SIDE) % count) for i in range(count)])


def add_replica(value, bit):
    count = lax.axis_size("rep")
    return value + lax.ppermute(value, "rep", [(i, i ^ bit) for i in range(count)])


def wide(value):
    return value.astype(jnp.float32)


def narrow(value):
    return value.astype(jnp.bfloat16)


def scatter_line(own, one, three, two, along):
    half = own.shape[0] // 2
    to_three = swap(two[:half], along, 1)
    to_one = swap(two[half:], along, 3)
    one = jnp.concatenate([one[:half], narrow(wide(one[half:]) + wide(to_one))], 0)
    three = jnp.concatenate([narrow(wide(three[:half]) + wide(to_three)), three[half:]], 0)
    return wide(own) + wide(swap(one, along, 1)) + wide(swap(three, along, 3))


def place_kernel(at_ref, source_ref, *token_refs):
    block = source_ref.shape[1] // (SIDE * SIDE)
    pair = 2 * block
    at_x = at_ref[0]
    at_z = at_ref[1]
    odd = at_z % 2

    def pair_of(slab, upper):
        slab = (at_x + slab + 2 * SIDE) % SIDE
        start = pl.multiple_of((slab * 2 + ((at_z // 2) ^ upper)) * pair, pair)
        return source_ref[:, pl.ds(start, pair)]

    def store(parity):
        def piece(slab, bits):
            first = (bits % 2) ^ parity == 0
            both = pair_of(slab, bits // 2)
            return both[:, :block] if first else both[:, block:]

        def put(ref, pieces):
            for place in range(2):
                two = [piece(*which) for which in pieces[2 * place : 2 * place + 2]]
                ref[:, place * pair : (place + 1) * pair] = jnp.concatenate(two, 1)

        for ref, slab in ((token_refs[0], 0), (token_refs[1], -1)):
            put(ref, ((slab, 0), (slab, 3), (slab - 1, 1), (slab - 1, 2)))
        for ref, slab in ((token_refs[2], 0), (token_refs[3], 1)):
            put(ref, ((slab, 1), (slab + 1, 0), (slab + 1, 3), (slab, 2)))

    @pl.when(odd == 0)
    def _():
        store(0)

    @pl.when(odd == 1)
    def _():
        store(1)


def place_tokens(at_x, at_z, source):
    tokens, width = source.shape
    whole = pl.BlockSpec(memory_space=pltpu.VMEM)
    return pl.pallas_call(
        place_kernel,
        out_shape=[jax.ShapeDtypeStruct((tokens, width // SIDE), source.dtype)] * SIDE,
        in_specs=[pl.BlockSpec(memory_space=pltpu.SMEM), whole],
        out_specs=[whole] * SIDE,
        compiler_params=pltpu.CompilerParams(vmem_limit_bytes=32 * 2**20),
        cost_estimate=pl.CostEstimate(
            flops=0, bytes_accessed=4 * tokens * width, transcendentals=0
        ),
    )(jnp.stack([at_x, at_z]).astype(jnp.int32), source)


def keep_kernel(*refs):
    for source_ref, to_ref in zip(refs[: len(refs) // 2], refs[len(refs) // 2 :]):
        to_ref[...] = source_ref[...]


def keep_near(*arrays):
    whole = pl.BlockSpec(memory_space=pltpu.VMEM)
    return pl.pallas_call(
        keep_kernel,
        out_shape=[jax.ShapeDtypeStruct(array.shape, array.dtype) for array in arrays],
        in_specs=[whole] * len(arrays),
        out_specs=[whole] * len(arrays),
        compiler_params=pltpu.CompilerParams(vmem_limit_bytes=32 * 2**20),
        cost_estimate=pl.CostEstimate(
            flops=0,
            bytes_accessed=4 * sum(array.size for array in arrays),
            transcendentals=0,
        ),
    )(*arrays)


def at_fragment(which, old, replaced):
    blocks = []
    for start in range(0, old.shape[1], HEAD_DIM):
        block = old[:, start : start + HEAD_DIM]
        blocks.append(jnp.where(which == start // HEAD_DIM, replaced(block), block))
    return jnp.concatenate(blocks, 1)


def mix_fragment(which, weight, new_anchor):
    return at_fragment(
        which, weight, lambda block: mixing * block + (1.0 - mixing) * new_anchor
    )


def shards(activations, cotangent, inner_weights, adam_m, adam_v, anchor, momentum, fragment):
    weight = inner_weights[0]
    first = adam_m[0]
    second = adam_v[0]
    rows = weight.shape[0]
    start_first = fragment[0] * HEAD_DIM
    start_second = fragment[1] * HEAD_DIM
    replicas = lax.axis_size("rep")
    place = lax.axis_index("fsdp")
    at_x = place // SIDE
    at_z = place % SIDE
    tie = lax.optimization_barrier

    working = weight.astype(jnp.bfloat16)
    working, activations, weight = tie((working, activations, weight))
    own_a, send_a, own_b, send_b = place_tokens(at_x, at_z, activations)
    working, send_a, send_b = tie((working, send_a, send_b))
    next_a = shift(send_a, -1)
    last_b = shift(send_b, 1)

    def product(chunk, whole):
        return lax.dot_general(
            chunk, whole, (((1,), (0,)), ((), ())), preferred_element_type=jnp.float32
        )

    def turned(chunk, key_grad):
        return lax.dot_general(
            chunk, key_grad, (((0,), (0,)), ((), ())), preferred_element_type=jnp.float32
        )

    def far_block(near, wrap):
        half = rows // 2
        return jnp.concatenate(
            [swap(wrap[:half], "z", 1), swap(near[half:], "z", 3)], 0
        )

    def parts_of_keys(rows_a, rows_b):
        from_last = shift(narrow(product(next_a, rows_a)), 1)
        from_next = shift(narrow(product(last_b, rows_b)), -1)
        return product(own_a, rows_a) + product(own_b, rows_b), from_last, from_next

    def gradient(keys):
        key_grad = normalize_back(keys, cotangent)
        next_grad = shift(key_grad, -1)
        last_grad = shift(key_grad, 1)
        grad_a = narrow(turned(own_a, key_grad) + turned(next_a, next_grad))
        far = shift(grad_a[3 * rows :], -1)
        grad_b = narrow(turned(own_b, key_grad) + turned(last_b, last_grad))
        near = shift(grad_a[2 * rows : 3 * rows], -1)
        own_wrap = shift(grad_b[rows : 3 * rows], 1)
        far = narrow(wide(grad_b[3 * rows :]) + wide(far))
        near = narrow(wide(grad_b[:rows]) + wide(near))
        own = narrow(wide(grad_a[:rows]) + wide(own_wrap[:rows]))
        wrap = narrow(wide(grad_a[rows : 2 * rows]) + wide(own_wrap[rows:]))
        return scatter_line(own, near, wrap, far, "z")

    near = swap(working, "z", 1)
    wrap = swap(working, "z", 3)
    total = two_blocks(weight, start_first, start_second)
    total = add_replica(add_replica(total, 1), 8)
    far = far_block(near, wrap)
    next_a, last_b, working, near, wrap, far, total = tie(
        (next_a, last_b, working, near, wrap, far, total)
    )
    total = add_replica(total, 2)
    next_a, last_b = keep_near(next_a, last_b)
    after = shift(jnp.concatenate([working, wrap], 0), -1)
    before = shift(jnp.concatenate([near, far], 0), 1)
    total, after, before, next_a, last_b = tie((total, after, before, next_a, last_b))
    total = add_replica(total, 4)
    keys, from_last, from_next = parts_of_keys(
        jnp.concatenate([working, wrap, before], 0),
        jnp.concatenate([near, after, far], 0),
    )
    total, from_last, from_next = tie((total, from_last, from_next))
    held = two_blocks(anchor, start_first, start_second)
    carried = two_blocks(momentum, start_first, start_second)
    new_anchor, new_carried = outer_update(held, carried, total, replicas)
    grad = gradient(keys + wide(from_last) + wide(from_next))
    weight, first, second = adamw(weight, first, second, grad)
    weight = mix_fragment(fragment[0], weight, new_anchor[:, :HEAD_DIM])
    working = weight.astype(jnp.bfloat16)
    near = swap(working, "z", 1)
    wrap = swap(working, "z", 3)
    after_own = shift(working, -1)
    far = far_block(near, wrap)
    after_wrap = shift(wrap, -1)
    before_near = shift(near, 1)
    before_far = shift(far, 1)
    keys, from_last, from_next = parts_of_keys(
        jnp.concatenate([working, wrap, before_near, before_far], 0),
        jnp.concatenate([near, after_own, after_wrap, far], 0),
    )
    grad = gradient(keys + wide(from_last) + wide(from_next))
    weight, first, second = adamw(weight, first, second, grad)
    weight = mix_fragment(fragment[1], weight, new_anchor[:, HEAD_DIM:])
    new_momentum = at_fragment(
        fragment[0], momentum, lambda block: new_carried[:, :HEAD_DIM]
    )
    new_momentum = at_fragment(
        fragment[1], new_momentum, lambda block: new_carried[:, HEAD_DIM:]
    )
    return (weight[None], new_momentum)


def solution(mesh):
    return jax.shard_map(
        shards,
        mesh=mesh,
        in_specs=(
            P(("rep", "fsdp"), None),
            P(("rep", "fsdp"), None),
            P("rep", "fsdp", None),
            P("rep", "fsdp", None),
            P("rep", "fsdp", None),
            P("fsdp", None),
            P("fsdp", None),
            P(),
        ),
        out_specs=(P("rep", "fsdp", None), P("fsdp", None)),
        check_vma=False,
    )
```

```python
import functools

import jax
import jax.numpy as jnp
from jax import lax
from jax.experimental import pallas as pl
from jax.experimental.pallas import tpu as pltpu
from jax.sharding import PartitionSpec as P

HEAD_DIM = 128
SIDE = 4


beta_first = 0.9
beta_second = 0.95
inner_rate = 0.1
decay_rate = 0.1
adam_epsilon = 1e-08
norm_epsilon = 1e-06
outer_rate = 0.7
nesterov = 0.9
mixing = 0.5


def outer_update(held, carried, total, replicas):
    delta = held - total / replicas
    carried = nesterov * carried + delta
    return (held - outer_rate * (delta + nesterov * carried), carried)


def normalize_back(keys, cotangent):
    scale = jnp.sqrt(jnp.mean(keys * keys, -1, keepdims=True) + norm_epsilon)
    normed = keys / scale
    upstream = cotangent.astype(jnp.float32)
    inner = jnp.mean(upstream * normed, -1, keepdims=True)
    return ((upstream - normed * inner) / scale).astype(jnp.bfloat16)


def adamw(weight, first, second, grad):
    first = beta_first * first + (1.0 - beta_first) * grad
    second = beta_second * second + (1.0 - beta_second) * grad * grad
    weight = weight - inner_rate * (first / (jnp.sqrt(second) + adam_epsilon) + decay_rate * weight)
    return (weight, first, second)


def two_blocks(source, start_first, start_second):
    return jnp.concatenate(
        [
            lax.dynamic_slice_in_dim(source, start_first, HEAD_DIM, 1),
            lax.dynamic_slice_in_dim(source, start_second, HEAD_DIM, 1),
        ],
        1,
    )


def swap(value, along, bits):
    step = bits * SIDE if along == "x" else bits
    return lax.ppermute(value, "fsdp", [(i, i ^ step) for i in range(SIDE * SIDE)])


def shift(value, step):
    count = SIDE * SIDE
    return lax.ppermute(value, "fsdp", [(i, (i + step * SIDE) % count) for i in range(count)])


def add_replica(value, bit):
    count = lax.axis_size("rep")
    return value + lax.ppermute(value, "rep", [(i, i ^ bit) for i in range(count)])


def wide(value):
    return value.astype(jnp.float32)


def narrow(value):
    return value.astype(jnp.bfloat16)


def scatter_line(own, one, three, two, along):
    half = own.shape[0] // 2
    to_three = swap(two[:half], along, 1)
    to_one = swap(two[half:], along, 3)
    one = jnp.concatenate([one[:half], narrow(wide(one[half:]) + wide(to_one))], 0)
    three = jnp.concatenate([narrow(wide(three[:half]) + wide(to_three)), three[half:]], 0)
    return wide(own) + wide(swap(one, along, 1)) + wide(swap(three, along, 3))


PIECES_A = ((0, 1), (0, 3), (-1, 0), (-1, 2))
PIECES_B = ((0, 0), (0, 2), (1, 1), (1, 3))


def place_kernel(from_x, slabs, at_ref, source_ref, a_ref, b_ref, held_ref, sem_ref):
    block = source_ref.shape[1] // (SIDE * SIDE)
    pair = 2 * block
    at_x = at_ref[0]
    at_z = at_ref[1]
    odd = at_z % 2
    copies = []
    for index, slab in enumerate(slabs):
        for upper in range(2):
            place = ((at_x + slab + SIDE) % SIDE) * 2 + ((at_z // 2) ^ upper)
            start = pl.multiple_of(place * pair, pair)
            to = (2 * index + upper) * pair
            copies.append(
                pltpu.make_async_copy(
                    source_ref.at[:, pl.ds(start, pair)],
                    held_ref.at[:, to : to + pair],
                    sem_ref.at[2 * index + upper],
                )
            )
    for copy in copies:
        copy.start()
    for copy in copies:
        copy.wait()

    def store(parity):
        def piece(base, which):
            slab, bits = which
            slab = (base + slab + 1) % SIDE - 1
            offset = (2 * slabs.index(slab) + bits // 2) * pair
            offset += block * ((bits % 2) ^ parity)
            return held_ref[:, offset : offset + block]

        a_ref[...] = jnp.concatenate([piece(-from_x, p) for p in PIECES_A], 1)
        b_ref[...] = jnp.concatenate([piece(from_x, p) for p in PIECES_B], 1)

    @pl.when(odd == 0)
    def _():
        store(0)

    @pl.when(odd == 1)
    def _():
        store(1)


def place_tokens(from_x, at, source):
    tokens, width = source.shape
    slabs = (-1, 0, 1) if from_x == 0 else (-1, 1, 2)
    whole = pl.BlockSpec(memory_space=pltpu.VMEM)
    return pl.pallas_call(
        functools.partial(place_kernel, from_x, slabs),
        out_shape=[jax.ShapeDtypeStruct((tokens, width // SIDE), source.dtype)] * 2,
        in_specs=[
            pl.BlockSpec(memory_space=pltpu.SMEM),
            pl.BlockSpec(memory_space=pltpu.HBM),
        ],
        out_specs=[whole] * 2,
        scratch_shapes=[
            pltpu.VMEM((tokens, len(slabs) * (width // SIDE)), source.dtype),
            pltpu.SemaphoreType.DMA((2 * len(slabs),)),
        ],
        compiler_params=pltpu.CompilerParams(vmem_limit_bytes=10 * 2**20),
        cost_estimate=pl.CostEstimate(
            flops=0, bytes_accessed=3 * tokens * width, transcendentals=0
        ),
    )(at, source)


def keep_kernel(a_ref, b_ref, to_a_ref, to_b_ref, sem_ref):
    copies = [
        pltpu.make_async_copy(a_ref, to_a_ref, sem_ref.at[0]),
        pltpu.make_async_copy(b_ref, to_b_ref, sem_ref.at[1]),
    ]
    for copy in copies:
        copy.start()
    for copy in copies:
        copy.wait()


def keep_near(a, b):
    return pl.pallas_call(
        keep_kernel,
        out_shape=[jax.ShapeDtypeStruct(array.shape, array.dtype) for array in (a, b)],
        in_specs=[pl.BlockSpec(memory_space=pl.ANY)] * 2,
        out_specs=[pl.BlockSpec(memory_space=pltpu.VMEM)] * 2,
        scratch_shapes=[pltpu.SemaphoreType.DMA((2,))],
        compiler_params=pltpu.CompilerParams(vmem_limit_bytes=10 * 2**20),
        cost_estimate=pl.CostEstimate(
            flops=0, bytes_accessed=4 * (a.size + b.size), transcendentals=0
        ),
    )(a, b)


def at_fragment(which, old, replaced):
    columns = old.shape[1]
    held = lax.broadcasted_iota(jnp.int32, (1, columns), 1) // HEAD_DIM == which
    return jnp.where(held, jnp.concatenate([replaced] * (columns // HEAD_DIM), 1), old)


def mix_fragment(which, weight, new_anchor):
    columns = weight.shape[1]
    held = lax.broadcasted_iota(jnp.int32, (1, columns), 1) // HEAD_DIM == which
    anchors = jnp.concatenate([new_anchor] * (columns // HEAD_DIM), 1)
    return jnp.where(held, mixing * weight + (1.0 - mixing) * anchors, weight)


def shards(activations, cotangent, inner_weights, adam_m, adam_v, anchor, momentum, fragment):
    weight = inner_weights[0]
    first = adam_m[0]
    second = adam_v[0]
    rows = weight.shape[0]
    start_first = fragment[0] * HEAD_DIM
    start_second = fragment[1] * HEAD_DIM
    replicas = lax.axis_size("rep")
    place = lax.axis_index("fsdp")
    at_x = place // SIDE
    at_z = place % SIDE
    tie = lax.optimization_barrier

    tie = lax.optimization_barrier

    at = jnp.stack([at_x, at_z]).astype(jnp.int32)
    send_a, send_b = place_tokens(1, at, activations)
    send_a, send_b, weight = tie((send_a, send_b, weight))
    next_a = shift(send_a, -1)
    last_b = shift(send_b, 1)
    working = weight.astype(jnp.bfloat16)

    def product(chunk, whole):
        return lax.dot_general(
            chunk, whole, (((1,), (0,)), ((), ())), preferred_element_type=jnp.float32
        )

    def turned(chunk, key_grad):
        return lax.dot_general(
            chunk, key_grad, (((0,), (0,)), ((), ())), preferred_element_type=jnp.float32
        )

    def far_block(near, wrap):
        half = rows // 2
        return jnp.concatenate(
            [swap(wrap[:half], "z", 1), swap(near[half:], "z", 3)], 0
        )

    def parts_of_keys(rows_a, rows_b):
        from_last = shift(narrow(product(next_a, rows_a)), 1)
        from_next = shift(narrow(product(last_b, rows_b)), -1)
        return product(own_a, rows_a) + product(own_b, rows_b), from_last, from_next

    def gradient(keys):
        key_grad = normalize_back(keys, cotangent)
        next_grad = shift(key_grad, -1)
        last_grad = shift(key_grad, 1)
        own_grad_a, own_grad_b = tie((turned(own_a, key_grad), turned(own_b, key_grad)))
        grad_a = narrow(own_grad_a + turned(next_a, next_grad))
        far = shift(grad_a[3 * rows :], -1)
        grad_b = narrow(own_grad_b + turned(last_b, last_grad))
        sides = shift(grad_b[2 * rows :], 1)
        own = shift(grad_a[2 * rows : 3 * rows], -1)
        far = narrow(wide(grad_b[rows : 2 * rows]) + wide(far))
        sides = narrow(wide(grad_a[: 2 * rows]) + wide(sides))
        own = narrow(wide(grad_b[:rows]) + wide(own))
        return scatter_line(own, sides[:rows], sides[rows:], far, "z")

    near = swap(working, "z", 1)
    wrap = swap(working, "z", 3)
    before_own = shift(working, 1)
    total = two_blocks(weight, start_first, start_second)
    near, wrap, before_own = tie((near, wrap, before_own))
    sides = jnp.concatenate([near, wrap], 0)
    after = shift(sides, -1)
    far = far_block(near, wrap)
    activations, far, total = tie((activations, far, total))
    own_a, own_b = place_tokens(0, at, activations)
    before_far = shift(far, 1)
    total = add_replica(add_replica(total, 1), 8)
    next_a, last_b = keep_near(next_a, last_b)
    before_far, own_a, own_b, total = tie((before_far, own_a, own_b, total))
    total = add_replica(total, 2)
    keys, from_last, from_next = parts_of_keys(
        jnp.concatenate([sides, before_own, before_far], 0),
        jnp.concatenate([working, far, after], 0),
    )
    total, from_last, from_next = tie((total, from_last, from_next))
    total = add_replica(total, 4)
    held = two_blocks(anchor, start_first, start_second)
    carried = two_blocks(momentum, start_first, start_second)
    new_anchor, new_carried = outer_update(held, carried, total, replicas)
    grad = gradient(keys + wide(from_last) + wide(from_next))
    weight, first, second = adamw(weight, first, second, grad)
    weight = mix_fragment(fragment[0], weight, new_anchor[:, :HEAD_DIM])
    working = weight.astype(jnp.bfloat16)
    near = swap(working, "z", 1)
    wrap = swap(working, "z", 3)
    before_own = shift(working, 1)
    far = far_block(near, wrap)
    sides = jnp.concatenate([near, wrap], 0)
    after = shift(sides, -1)
    before_far = shift(far, 1)
    keys, from_last, from_next = parts_of_keys(
        jnp.concatenate([sides, before_own, before_far], 0),
        jnp.concatenate([working, far, after], 0),
    )
    grad = gradient(keys + wide(from_last) + wide(from_next))
    weight, first, second = adamw(weight, first, second, grad)
    weight = mix_fragment(fragment[1], weight, new_anchor[:, HEAD_DIM:])
    new_momentum = at_fragment(fragment[0], momentum, new_carried[:, :HEAD_DIM])
    new_momentum = at_fragment(fragment[1], new_momentum, new_carried[:, HEAD_DIM:])
    return (weight[None], new_momentum)


def solution(mesh):
    return jax.shard_map(
        shards,
        mesh=mesh,
        in_specs=(
            P(("rep", "fsdp"), None),
            P(("rep", "fsdp"), None),
            P("rep", "fsdp", None),
            P("rep", "fsdp", None),
            P("rep", "fsdp", None),
            P("fsdp", None),
            P("fsdp", None),
            P(),
        ),
        out_specs=(P("rep", "fsdp", None), P("fsdp", None)),
        check_vma=False,
    )
```

```python
import functools

import jax
import jax.numpy as jnp
from jax import lax
from jax.experimental import pallas as pl
from jax.experimental.pallas import tpu as pltpu
from jax.sharding import PartitionSpec as P

HEAD_DIM = 128
SIDE = 4


beta_first = 0.9
beta_second = 0.95
inner_rate = 0.1
decay_rate = 0.1
adam_epsilon = 1e-08
norm_epsilon = 1e-06
outer_rate = 0.7
nesterov = 0.9
mixing = 0.5


def outer_update(held, carried, total, replicas):
    delta = held - total / replicas
    carried = nesterov * carried + delta
    return (held - outer_rate * (delta + nesterov * carried), carried)


def normalize_back(keys, cotangent):
    scale = jnp.sqrt(jnp.mean(keys * keys, -1, keepdims=True) + norm_epsilon)
    normed = keys / scale
    upstream = cotangent.astype(jnp.float32)
    inner = jnp.mean(upstream * normed, -1, keepdims=True)
    return ((upstream - normed * inner) / scale).astype(jnp.bfloat16)


def adamw(weight, first, second, grad):
    first = beta_first * first + (1.0 - beta_first) * grad
    second = beta_second * second + (1.0 - beta_second) * grad * grad
    weight = weight - inner_rate * (first / (jnp.sqrt(second) + adam_epsilon) + decay_rate * weight)
    return (weight, first, second)


def two_blocks(source, start_first, start_second):
    return jnp.concatenate(
        [
            lax.dynamic_slice_in_dim(source, start_first, HEAD_DIM, 1),
            lax.dynamic_slice_in_dim(source, start_second, HEAD_DIM, 1),
        ],
        1,
    )


def swap(value, along, bits):
    step = bits * SIDE if along == "x" else bits
    return lax.ppermute(value, "fsdp", [(i, i ^ step) for i in range(SIDE * SIDE)])


def shift(value, step):
    count = SIDE * SIDE
    return lax.ppermute(value, "fsdp", [(i, (i + step * SIDE) % count) for i in range(count)])


def add_replica(value, bit):
    count = lax.axis_size("rep")
    return value + lax.ppermute(value, "rep", [(i, i ^ bit) for i in range(count)])


def wide(value):
    return value.astype(jnp.float32)


def narrow(value):
    return value.astype(jnp.bfloat16)


def scatter_line(own, one, three, two, along):
    half = own.shape[0] // 2
    to_three = swap(two[:half], along, 1)
    to_one = swap(two[half:], along, 3)
    one = jnp.concatenate([one[:half], narrow(wide(one[half:]) + wide(to_one))], 0)
    three = jnp.concatenate([narrow(wide(three[:half]) + wide(to_three)), three[half:]], 0)
    return wide(own) + wide(swap(one, along, 1)) + wide(swap(three, along, 3))


PIECES_A = ((0, 1), (0, 3), (-1, 0), (-1, 2))
PIECES_B = ((0, 0), (0, 2), (1, 1), (1, 3))


def place_kernel(from_x, slabs, at_ref, source_ref, a_ref, b_ref, held_ref, sem_ref):
    block = source_ref.shape[1] // (SIDE * SIDE)
    pair = 2 * block
    at_x = at_ref[0]
    at_z = at_ref[1]
    odd = at_z % 2
    copies = []
    for index, slab in enumerate(slabs):
        for upper in range(2):
            place = ((at_x + slab + SIDE) % SIDE) * 2 + ((at_z // 2) ^ upper)
            start = pl.multiple_of(place * pair, pair)
            to = (2 * index + upper) * pair
            copies.append(
                pltpu.make_async_copy(
                    source_ref.at[:, pl.ds(start, pair)],
                    held_ref.at[:, to : to + pair],
                    sem_ref.at[2 * index + upper],
                )
            )
    for copy in copies:
        copy.start()
    for copy in copies:
        copy.wait()

    def store(parity):
        def piece(base, which):
            slab, bits = which
            slab = (base + slab + 1) % SIDE - 1
            offset = (2 * slabs.index(slab) + bits // 2) * pair
            offset += block * ((bits % 2) ^ parity)
            return held_ref[:, offset : offset + block]

        a_ref[...] = jnp.concatenate([piece(-from_x, p) for p in PIECES_A], 1)
        b_ref[...] = jnp.concatenate([piece(from_x, p) for p in PIECES_B], 1)

    @pl.when(odd == 0)
    def _():
        store(0)

    @pl.when(odd == 1)
    def _():
        store(1)


def place_tokens(from_x, at, source):
    tokens, width = source.shape
    slabs = (-1, 0, 1) if from_x == 0 else (-1, 1, 2)
    whole = pl.BlockSpec(memory_space=pltpu.VMEM)
    return pl.pallas_call(
        functools.partial(place_kernel, from_x, slabs),
        out_shape=[jax.ShapeDtypeStruct((tokens, width // SIDE), source.dtype)] * 2,
        in_specs=[
            pl.BlockSpec(memory_space=pltpu.SMEM),
            pl.BlockSpec(memory_space=pltpu.HBM),
        ],
        out_specs=[whole] * 2,
        scratch_shapes=[
            pltpu.VMEM((tokens, len(slabs) * (width // SIDE)), source.dtype),
            pltpu.SemaphoreType.DMA((2 * len(slabs),)),
        ],
        compiler_params=pltpu.CompilerParams(vmem_limit_bytes=10 * 2**20),
        cost_estimate=pl.CostEstimate(
            flops=0, bytes_accessed=3 * tokens * width, transcendentals=0
        ),
    )(at, source)


def keep_kernel(a_ref, b_ref, to_a_ref, to_b_ref, sem_ref):
    copies = [
        pltpu.make_async_copy(a_ref, to_a_ref, sem_ref.at[0]),
        pltpu.make_async_copy(b_ref, to_b_ref, sem_ref.at[1]),
    ]
    for copy in copies:
        copy.start()
    for copy in copies:
        copy.wait()


def keep_near(a, b):
    return pl.pallas_call(
        keep_kernel,
        out_shape=[jax.ShapeDtypeStruct(array.shape, array.dtype) for array in (a, b)],
        in_specs=[pl.BlockSpec(memory_space=pl.ANY)] * 2,
        out_specs=[pl.BlockSpec(memory_space=pltpu.VMEM)] * 2,
        scratch_shapes=[pltpu.SemaphoreType.DMA((2,))],
        compiler_params=pltpu.CompilerParams(vmem_limit_bytes=10 * 2**20),
        cost_estimate=pl.CostEstimate(
            flops=0, bytes_accessed=4 * (a.size + b.size), transcendentals=0
        ),
    )(a, b)


def at_fragment(which, old, replaced):
    columns = old.shape[1]
    held = lax.broadcasted_iota(jnp.int32, (1, columns), 1) // HEAD_DIM == which
    return jnp.where(held, jnp.concatenate([replaced] * (columns // HEAD_DIM), 1), old)


def mix_fragment(which, weight, new_anchor):
    columns = weight.shape[1]
    held = lax.broadcasted_iota(jnp.int32, (1, columns), 1) // HEAD_DIM == which
    anchors = jnp.concatenate([new_anchor] * (columns // HEAD_DIM), 1)
    return jnp.where(held, mixing * weight + (1.0 - mixing) * anchors, weight)


def shards(activations, cotangent, inner_weights, adam_m, adam_v, anchor, momentum, fragment):
    weight = inner_weights[0]
    first = adam_m[0]
    second = adam_v[0]
    rows = weight.shape[0]
    start_first = fragment[0] * HEAD_DIM
    start_second = fragment[1] * HEAD_DIM
    replicas = lax.axis_size("rep")
    place = lax.axis_index("fsdp")
    at_x = place // SIDE
    at_z = place % SIDE
    tie = lax.optimization_barrier

    tie = lax.optimization_barrier

    at = jnp.stack([at_x, at_z]).astype(jnp.int32)
    send_a, send_b = place_tokens(1, at, activations)
    next_a = shift(send_a, -1)
    last_b = shift(send_b, 1)
    working = weight.astype(jnp.bfloat16)

    def product(chunk, whole):
        return lax.dot_general(
            chunk, whole, (((1,), (0,)), ((), ())), preferred_element_type=jnp.float32
        )

    def turned(chunk, key_grad):
        return lax.dot_general(
            chunk, key_grad, (((0,), (0,)), ((), ())), preferred_element_type=jnp.float32
        )

    def far_block(near, wrap):
        half = rows // 2
        return jnp.concatenate(
            [swap(wrap[:half], "z", 1), swap(near[half:], "z", 3)], 0
        )

    def parts_of_keys(rows_a, rows_b):
        from_last = shift(narrow(product(next_a, rows_a)), 1)
        from_next = shift(narrow(product(last_b, rows_b)), -1)
        return product(own_a, rows_a) + product(own_b, rows_b), from_last, from_next

    def gradient(keys, beside):
        key_grad = normalize_back(keys, cotangent)
        next_grad = shift(key_grad, -1)
        last_grad = shift(key_grad, 1)
        own_grad_a, own_grad_b = tie((turned(own_a, key_grad), turned(own_b, key_grad)))
        next_grad, beside = tie((next_grad, beside))
        grad_a = narrow(own_grad_a + turned(next_a, next_grad))
        far = shift(grad_a[3 * rows :], -1)
        grad_b = narrow(own_grad_b + turned(last_b, last_grad))
        sides = shift(grad_b[2 * rows :], 1)
        own, far = tie((grad_a[2 * rows : 3 * rows], far))
        own = shift(own, -1)
        far = narrow(wide(grad_b[rows : 2 * rows]) + wide(far))
        sides = narrow(wide(grad_a[: 2 * rows]) + wide(sides))
        own = narrow(wide(grad_b[:rows]) + wide(own))
        return scatter_line(own, sides[:rows], sides[rows:], far, "z"), beside

    near = swap(working, "z", 1)
    wrap = swap(working, "z", 3)
    before_own = shift(working, 1)
    total = two_blocks(weight, start_first, start_second)
    near, wrap, before_own = tie((near, wrap, before_own))
    sides = jnp.concatenate([near, wrap], 0)
    after = shift(sides, -1)
    far = far_block(near, wrap)
    activations, far, total = tie((activations, far, total))
    own_a, own_b = place_tokens(0, at, activations)
    before_far = shift(far, 1)
    total = add_replica(add_replica(total, 1), 8)
    next_a, last_b = keep_near(next_a, last_b)
    before_far, own_a, own_b, total = tie((before_far, own_a, own_b, total))
    total = add_replica(total, 2)
    keys, from_last, from_next = parts_of_keys(
        jnp.concatenate([sides, before_own, before_far], 0),
        jnp.concatenate([working, far, after], 0),
    )
    total, from_last, from_next = tie((total, from_last, from_next))
    total = add_replica(total, 4)
    grad, total = gradient(keys + wide(from_last) + wide(from_next), total)
    held = two_blocks(anchor, start_first, start_second)
    carried = two_blocks(momentum, start_first, start_second)
    new_anchor, new_carried = outer_update(held, carried, total, replicas)
    weight, first, second = adamw(weight, first, second, grad)
    weight = mix_fragment(fragment[0], weight, new_anchor[:, :HEAD_DIM])
    working = weight.astype(jnp.bfloat16)
    near = swap(working, "z", 1)
    wrap = swap(working, "z", 3)
    before_own = shift(working, 1)
    far = far_block(near, wrap)
    sides = jnp.concatenate([near, wrap], 0)
    after = shift(sides, -1)
    before_far = shift(far, 1)
    keys, from_last, from_next = parts_of_keys(
        jnp.concatenate([sides, before_own, before_far], 0),
        jnp.concatenate([working, far, after], 0),
    )
    grad, new_anchor = gradient(keys + wide(from_last) + wide(from_next), new_anchor)
    weight, first, second = adamw(weight, first, second, grad)
    weight = mix_fragment(fragment[1], weight, new_anchor[:, HEAD_DIM:])
    new_momentum = at_fragment(fragment[0], momentum, new_carried[:, :HEAD_DIM])
    new_momentum = at_fragment(fragment[1], new_momentum, new_carried[:, HEAD_DIM:])
    return (weight[None], new_momentum)


def solution(mesh):
    return jax.shard_map(
        shards,
        mesh=mesh,
        in_specs=(
            P(("rep", "fsdp"), None),
            P(("rep", "fsdp"), None),
            P("rep", "fsdp", None),
            P("rep", "fsdp", None),
            P("rep", "fsdp", None),
            P("fsdp", None),
            P("fsdp", None),
            P(),
        ),
        out_specs=(P("rep", "fsdp", None), P("fsdp", None)),
        check_vma=False,
    )
```

```python
import functools

import jax
import jax.numpy as jnp
from jax import lax
from jax.experimental import pallas as pl
from jax.experimental.pallas import tpu as pltpu
from jax.sharding import PartitionSpec as P

HEAD_DIM = 128
SIDE = 4


beta_first = 0.9
beta_second = 0.95
inner_rate = 0.1
decay_rate = 0.1
adam_epsilon = 1e-08
norm_epsilon = 1e-06
outer_rate = 0.7
nesterov = 0.9
mixing = 0.5


def outer_update(held, carried, total, replicas):
    delta = held - total / replicas
    carried = nesterov * carried + delta
    return (held - outer_rate * (delta + nesterov * carried), carried)


def normalize_back(keys, cotangent):
    scale = jnp.sqrt(jnp.mean(keys * keys, -1, keepdims=True) + norm_epsilon)
    normed = keys / scale
    upstream = cotangent.astype(jnp.float32)
    inner = jnp.mean(upstream * normed, -1, keepdims=True)
    return ((upstream - normed * inner) / scale).astype(jnp.bfloat16)


def adamw(weight, first, second, grad):
    first = beta_first * first + (1.0 - beta_first) * grad
    second = beta_second * second + (1.0 - beta_second) * grad * grad
    weight = weight - inner_rate * (first / (jnp.sqrt(second) + adam_epsilon) + decay_rate * weight)
    return (weight, first, second)


def two_blocks(source, start_first, start_second):
    return jnp.concatenate(
        [
            lax.dynamic_slice_in_dim(source, start_first, HEAD_DIM, 1),
            lax.dynamic_slice_in_dim(source, start_second, HEAD_DIM, 1),
        ],
        1,
    )


def swap(value, along, bits):
    step = bits * SIDE if along == "x" else bits
    return lax.ppermute(value, "fsdp", [(i, i ^ step) for i in range(SIDE * SIDE)])


def shift(value, step):
    count = SIDE * SIDE
    return lax.ppermute(value, "fsdp", [(i, (i + step * SIDE) % count) for i in range(count)])


def add_replica(value, bit):
    count = lax.axis_size("rep")
    return value + lax.ppermute(value, "rep", [(i, i ^ bit) for i in range(count)])


def wide(value):
    return value.astype(jnp.float32)


def narrow(value):
    return value.astype(jnp.bfloat16)


def scatter_line(own, one, three, two, along):
    half = own.shape[0] // 2
    to_three = swap(two[:half], along, 1)
    to_one = swap(two[half:], along, 3)
    one = jnp.concatenate([one[:half], narrow(wide(one[half:]) + wide(to_one))], 0)
    three = jnp.concatenate([narrow(wide(three[:half]) + wide(to_three)), three[half:]], 0)
    return wide(own) + wide(swap(one, along, 1)) + wide(swap(three, along, 3))


PIECES_A = ((0, 1), (0, 3), (-1, 0), (-1, 2))
PIECES_B = ((0, 0), (0, 2), (1, 1), (1, 3))


def place_kernel(from_x, at_ref, source_ref, a_ref, b_ref):
    block = source_ref.shape[1] // (SIDE * SIDE)
    pair = 2 * block
    at_x = at_ref[0]
    at_z = at_ref[1]
    odd = at_z % 2

    def store(parity):
        def piece(base, which):
            slab, bits = which
            slab = (at_x + base + slab + SIDE) % SIDE
            place = pl.multiple_of((slab * 2 + ((at_z // 2) ^ (bits // 2))) * pair, pair)
            offset = block * ((bits % 2) ^ parity)
            return source_ref[:, pl.ds(place, pair)][:, offset : offset + block]

        a_ref[...] = jnp.concatenate([piece(-from_x, p) for p in PIECES_A], 1)
        b_ref[...] = jnp.concatenate([piece(from_x, p) for p in PIECES_B], 1)

    @pl.when(odd == 0)
    def _():
        store(0)

    @pl.when(odd == 1)
    def _():
        store(1)


def place_tokens(from_x, at, source):
    tokens, width = source.shape
    whole = pl.BlockSpec(memory_space=pltpu.VMEM)
    return pl.pallas_call(
        functools.partial(place_kernel, from_x),
        out_shape=[jax.ShapeDtypeStruct((tokens, width // SIDE), source.dtype)] * 2,
        in_specs=[pl.BlockSpec(memory_space=pltpu.SMEM), whole],
        out_specs=[whole] * 2,
        compiler_params=pltpu.CompilerParams(vmem_limit_bytes=12 * 2**20),
        cost_estimate=pl.CostEstimate(
            flops=0, bytes_accessed=3 * tokens * width, transcendentals=0
        ),
    )(at, source)


def keep_kernel(a_ref, b_ref, to_a_ref, to_b_ref, sem_ref):
    copies = [
        pltpu.make_async_copy(a_ref, to_a_ref, sem_ref.at[0]),
        pltpu.make_async_copy(b_ref, to_b_ref, sem_ref.at[1]),
    ]
    for copy in copies:
        copy.start()
    for copy in copies:
        copy.wait()


def keep_near(a, b):
    return pl.pallas_call(
        keep_kernel,
        out_shape=[jax.ShapeDtypeStruct(array.shape, array.dtype) for array in (a, b)],
        in_specs=[pl.BlockSpec(memory_space=pl.ANY)] * 2,
        out_specs=[pl.BlockSpec(memory_space=pltpu.VMEM)] * 2,
        scratch_shapes=[pltpu.SemaphoreType.DMA((2,))],
        compiler_params=pltpu.CompilerParams(vmem_limit_bytes=10 * 2**20),
        cost_estimate=pl.CostEstimate(
            flops=0, bytes_accessed=4 * (a.size + b.size), transcendentals=0
        ),
    )(a, b)


def at_fragment(which, old, replaced):
    columns = old.shape[1]
    held = lax.broadcasted_iota(jnp.int32, (1, columns), 1) // HEAD_DIM == which
    return jnp.where(held, jnp.concatenate([replaced] * (columns // HEAD_DIM), 1), old)


def mix_fragment(which, weight, new_anchor):
    columns = weight.shape[1]
    held = lax.broadcasted_iota(jnp.int32, (1, columns), 1) // HEAD_DIM == which
    anchors = jnp.concatenate([new_anchor] * (columns // HEAD_DIM), 1)
    return jnp.where(held, mixing * weight + (1.0 - mixing) * anchors, weight)


def shards(activations, cotangent, inner_weights, adam_m, adam_v, anchor, momentum, fragment):
    weight = inner_weights[0]
    first = adam_m[0]
    second = adam_v[0]
    rows = weight.shape[0]
    start_first = fragment[0] * HEAD_DIM
    start_second = fragment[1] * HEAD_DIM
    replicas = lax.axis_size("rep")
    place = lax.axis_index("fsdp")
    at_x = place // SIDE
    at_z = place % SIDE
    tie = lax.optimization_barrier

    tie = lax.optimization_barrier

    at = jnp.stack([at_x, at_z]).astype(jnp.int32)
    send_a, send_b = place_tokens(1, at, activations)
    next_a = shift(send_a, -1)
    last_b = shift(send_b, 1)
    working = weight.astype(jnp.bfloat16)

    def product(chunk, whole):
        return lax.dot_general(
            chunk, whole, (((1,), (0,)), ((), ())), preferred_element_type=jnp.float32
        )

    def turned(chunk, key_grad):
        return lax.dot_general(
            chunk, key_grad, (((0,), (0,)), ((), ())), preferred_element_type=jnp.float32
        )

    def far_block(near, wrap):
        half = rows // 2
        return jnp.concatenate(
            [swap(wrap[:half], "z", 1), swap(near[half:], "z", 3)], 0
        )

    def parts_of_keys(rows_a, rows_b):
        from_last = shift(narrow(product(next_a, rows_a)), 1)
        from_next = shift(narrow(product(last_b, rows_b)), -1)
        return product(own_a, rows_a) + product(own_b, rows_b), from_last, from_next

    def gradient(keys, beside):
        key_grad = normalize_back(keys, cotangent)
        next_grad = shift(key_grad, -1)
        last_grad = shift(key_grad, 1)
        own_grad_a, own_grad_b = tie((turned(own_a, key_grad), turned(own_b, key_grad)))
        next_grad, beside = tie((next_grad, beside))
        grad_a = narrow(own_grad_a + turned(next_a, next_grad))
        far = shift(grad_a[3 * rows :], -1)
        grad_b = narrow(own_grad_b + turned(last_b, last_grad))
        sides = shift(grad_b[2 * rows :], 1)
        own, far = tie((grad_a[2 * rows : 3 * rows], far))
        own = shift(own, -1)
        far = narrow(wide(grad_b[rows : 2 * rows]) + wide(far))
        sides = narrow(wide(grad_a[: 2 * rows]) + wide(sides))
        own = narrow(wide(grad_b[:rows]) + wide(own))
        return scatter_line(own, sides[:rows], sides[rows:], far, "z"), beside

    near = swap(working, "z", 1)
    wrap = swap(working, "z", 3)
    before_own = shift(working, 1)
    total = two_blocks(weight, start_first, start_second)
    near, wrap, before_own = tie((near, wrap, before_own))
    sides = jnp.concatenate([near, wrap], 0)
    after = shift(sides, -1)
    far = far_block(near, wrap)
    activations, far, total = tie((activations, far, total))
    own_a, own_b = place_tokens(0, at, activations)
    before_far = shift(far, 1)
    total = add_replica(add_replica(total, 1), 8)
    next_a, last_b = keep_near(next_a, last_b)
    before_far, own_a, own_b, total = tie((before_far, own_a, own_b, total))
    total = add_replica(total, 2)
    keys, from_last, from_next = parts_of_keys(
        jnp.concatenate([sides, before_own, before_far], 0),
        jnp.concatenate([working, far, after], 0),
    )
    total, from_last, from_next = tie((total, from_last, from_next))
    total = add_replica(total, 4)
    grad, total = gradient(keys + wide(from_last) + wide(from_next), total)
    held = two_blocks(anchor, start_first, start_second)
    carried = two_blocks(momentum, start_first, start_second)
    new_anchor, new_carried = outer_update(held, carried, total, replicas)
    weight, first, second = adamw(weight, first, second, grad)
    weight = mix_fragment(fragment[0], weight, new_anchor[:, :HEAD_DIM])
    working = weight.astype(jnp.bfloat16)
    near = swap(working, "z", 1)
    wrap = swap(working, "z", 3)
    before_own = shift(working, 1)
    far = far_block(near, wrap)
    sides = jnp.concatenate([near, wrap], 0)
    after = shift(sides, -1)
    before_far = shift(far, 1)
    keys, from_last, from_next = parts_of_keys(
        jnp.concatenate([sides, before_own, before_far], 0),
        jnp.concatenate([working, far, after], 0),
    )
    grad, new_anchor = gradient(keys + wide(from_last) + wide(from_next), new_anchor)
    weight, first, second = adamw(weight, first, second, grad)
    weight = mix_fragment(fragment[1], weight, new_anchor[:, HEAD_DIM:])
    new_momentum = at_fragment(fragment[0], momentum, new_carried[:, :HEAD_DIM])
    new_momentum = at_fragment(fragment[1], new_momentum, new_carried[:, HEAD_DIM:])
    return (weight[None], new_momentum)


def solution(mesh):
    return jax.shard_map(
        shards,
        mesh=mesh,
        in_specs=(
            P(("rep", "fsdp"), None),
            P(("rep", "fsdp"), None),
            P("rep", "fsdp", None),
            P("rep", "fsdp", None),
            P("rep", "fsdp", None),
            P("fsdp", None),
            P("fsdp", None),
            P(),
        ),
        out_specs=(P("rep", "fsdp", None), P("fsdp", None)),
        check_vma=False,
    )
```
